512 devices in a mesh: queue: 32 (over z_hi, x, core), sp: 16 (over z_lo, y).
Axes of the slice: x: 4, y: 4, z: 16 (z_hi: 4, z_lo: 4; z = z_hi * 4 + z_lo), core: 2. Of those that a mesh axis runs over, the one named last changes fastest.
Arguments:
- spatial_qkv: bfloat16 [64, 3, 2048, 1152], P('queue', None, 'sp'), may hold values from -8 to 8
- temporal_query: bfloat16 [64, 2048, 1152], P('queue', 'sp'), may hold values from -8 to 8
- temporal_kv: bfloat16 [64, 2, 2048, 1152], P('queue', None, 'sp'), may hold values from -8 to 8
- timestep: int32 [64], P('queue'), may hold values from 0 to 29
- noise_level: int32 [64], P('queue'), may hold values from 0 to 63
- spatial_gate: float32 [30, 1152], replicated, may hold values from 1 to 10
- temporal_gate: float32 [30, 1152], replicated, may hold values from 0.1 to 1
- step_table: float32 [64], replicated, may hold values from 0.5 to 2
Outputs:
- advanced: bfloat16 [64, 2048, 1152], P('queue', 'sp')
The draws below stay inside these ranges and needn't reach their ends.
All inputs are finite; a program needn't handle non-finite values.
Results may differ from the reference program's by a relative error of at most 0.0055.
Values may be sent and summed in bfloat16 or wider, within the bound.
No kernel may reach another device: no remote copies, remote signals or barrier semaphores. Data moves between devices by JAX's collectives and lax.ppermute only.
A program may use at most 64 MiB of HBM per device.

```python
import math
import jax
import jax.numpy as jnp
from jax import lax

D = 1152
HEADS = 16
HEAD_DIM = 72
PLEN = 16
NSTEPS = 30
LEVELS = 64
FRAMES = 64
FTOK = 2048
NPART = 4


def draw_spatial_qkv(key, part):
    key = jax.random.fold_in(key, 11)
    base_key = jax.random.fold_in(key, 0)
    values = jnp.clip(jax.random.normal(base_key, (FRAMES, 3, FTOK, D), jnp.float32), -6.0, 6.0)
    return values.astype(jnp.bfloat16)


def draw_temporal_query(key, part):
    key = jax.random.fold_in(key, 12)
    values = jnp.clip(jax.random.normal(key, (FRAMES, FTOK, D), jnp.float32), -6.0, 6.0)
    return values.astype(jnp.bfloat16)


def draw_temporal_kv(key, part):
    key = jax.random.fold_in(key, 13)
    values = jnp.clip(jax.random.normal(key, (FRAMES, 2, FTOK, D), jnp.float32), -6.0, 6.0)
    return values.astype(jnp.bfloat16)


def set_ends(values, stream_key, least, high):
    extent = values.shape
    place = [jax.random.randint(jax.random.fold_in(stream_key, axis), (), 0, extent[axis]) for axis in range(len(extent))]
    values = values.at[tuple(place)].set(least)
    longest = extent.index(max(extent))
    place[longest] = (place[longest] + 1) % extent[longest]
    return values.at[tuple(place)].set(high)


def setup_inputs(seed: int = 0) -> dict:
    seeds = jax.random.split(jax.random.key(seed), 9)
    return {
        "spatial_qkv": draw_spatial_qkv(jax.random.fold_in(seeds[8], 71), 0),
        "temporal_query": draw_temporal_query(jax.random.fold_in(seeds[8], 71), 0),
        "temporal_kv": draw_temporal_kv(jax.random.fold_in(seeds[8], 71), 0),
        "timestep": set_ends(jax.random.randint(seeds[3], (FRAMES,), 0, NSTEPS), jax.random.fold_in(seeds[3], 1), 0, NSTEPS - 1).astype(jnp.int32),
        "noise_level": set_ends(jax.random.randint(seeds[4], (FRAMES,), 0, LEVELS), jax.random.fold_in(seeds[4], 1), 0, LEVELS - 1).astype(jnp.int32),
        "spatial_gate": jnp.clip(jnp.exp(jax.random.uniform(seeds[5], (NSTEPS, D), jnp.float32, math.log(1.0), math.log(10.0))), 1.0, 10.0),
        "temporal_gate": jnp.clip(jnp.exp(jax.random.uniform(seeds[6], (NSTEPS, D), jnp.float32, math.log(0.1), math.log(1.0))), 0.1, 1.0),
        "step_table": jnp.clip(jnp.exp(jax.random.uniform(seeds[7], (LEVELS,), jnp.float32, math.log(0.5), math.log(2.0))), 0.5, 2.0),
    }


def spatial_frame(packed):
    query_all = packed[0].astype(jnp.float32).reshape(FTOK, HEADS, HEAD_DIM)
    key_all = packed[1].astype(jnp.float32).reshape(FTOK, HEADS, HEAD_DIM)
    value_all = packed[2].astype(jnp.float32).reshape(FTOK, HEADS, HEAD_DIM)
    block_rows = min(512, FTOK)
    score_scale = 1.0 / math.sqrt(HEAD_DIM)

    def one_block(block_index):
        query_rows = lax.dynamic_slice_in_dim(query_all, block_index * block_rows, block_rows, 0)
        scores = jnp.einsum('qhe,khe->hqk', query_rows, key_all) * score_scale
        row_max = lax.optimization_barrier(jnp.max(scores, axis=-1, keepdims=True))
        weights = jnp.exp(scores - row_max)
        row_sum = lax.optimization_barrier(jnp.sum(weights, axis=-1))
        rounded = lax.optimization_barrier(weights.astype(jnp.bfloat16)).astype(jnp.float32)
        weighted = jnp.einsum('hqk,khe->qhe', rounded, value_all)
        return (weighted / jnp.transpose(row_sum)[:, :, None]).astype(jnp.bfloat16)
    outputs = lax.map(one_block, jnp.arange(FTOK // block_rows, dtype=jnp.int32))
    return outputs.reshape(FTOK, D)

def temporal_part(pieces):
    query_part, kv_part = pieces
    score_scale = 1.0 / math.sqrt(HEAD_DIM)
    query_heads = query_part.astype(jnp.float32).reshape(PLEN, FTOK, HEADS, HEAD_DIM)
    key_heads = kv_part[:, 0].astype(jnp.float32).reshape(PLEN, FTOK, HEADS, HEAD_DIM)
    value_heads = kv_part[:, 1].astype(jnp.float32).reshape(PLEN, FTOK, HEADS, HEAD_DIM)
    scores = jnp.einsum('flhe,glhe->lhfg', query_heads, key_heads) * score_scale
    row_max = lax.optimization_barrier(jnp.max(scores, axis=-1, keepdims=True))
    weights = jnp.exp(scores - row_max)
    row_sum = lax.optimization_barrier(jnp.sum(weights, axis=-1))
    rounded = lax.optimization_barrier(weights.astype(jnp.bfloat16)).astype(jnp.float32)
    weighted = jnp.einsum('lhfg,glhe->flhe', rounded, value_heads)
    return (weighted / jnp.transpose(row_sum, (2, 0, 1))[..., None]).astype(jnp.bfloat16).reshape(PLEN, FTOK, D)

def reference(spatial_qkv, temporal_query, temporal_kv, timestep, noise_level, spatial_gate, temporal_gate, step_table):
    spatial_out = lax.map(spatial_frame, spatial_qkv)
    query_parts = temporal_query.reshape(NPART, PLEN, FTOK, D)
    kv_parts = temporal_kv.reshape(NPART, PLEN, 2, FTOK, D)
    temporal_out = lax.map(temporal_part, (query_parts, kv_parts)).reshape(FRAMES, FTOK, D)
    gate_space = spatial_gate[timestep]
    gate_time = temporal_gate[timestep]
    step_size = step_table[noise_level]
    space_out = lax.optimization_barrier(spatial_out).astype(jnp.float32)
    timely = lax.optimization_barrier(temporal_out).astype(jnp.float32)
    updated = (step_size[:, None, None] * (gate_space[:, None, :] * space_out + gate_time[:, None, :] * timely)).astype(jnp.bfloat16)
    return jnp.roll(updated, -1, axis=0)
```

```python
import math

import jax
import jax.numpy as jnp
from jax import lax
from jax.experimental import pallas as pl
from jax.experimental.pallas import tpu as pltpu
from jax.sharding import Mesh
from jax.sharding import PartitionSpec as P

D = 1152
HEADS = 16
HEAD_DIM = 72
PLEN = 16
GROUPS = 16
TOK = 128
QBLOCK = 256
SHARE = 16
SCALE = math.log2(math.e) / math.sqrt(HEAD_DIM)

F32 = jnp.float32
BF16 = jnp.bfloat16
VMEM = pl.BlockSpec(memory_space=pltpu.VMEM)
SMEM = pl.BlockSpec(memory_space=pltpu.SMEM)
PARAMS = pltpu.CompilerParams(vmem_limit_bytes=56 << 20)


def matmul(a, b, a_dim, b_dim):
    return lax.dot_general(
        a, b, (((a_dim,), (b_dim,)), ((), ())), preferred_element_type=F32
    )


def pack_kernel(x_ref, o_ref):
    for part in range(3):
        turned = x_ref[0, part].T
        for head in range(HEADS):
            o_ref[head, part] = turned[head * HEAD_DIM : (head + 1) * HEAD_DIM]


def pack_frame(spatial_qkv, frame):
    return pl.pallas_call(
        pack_kernel,
        grid=(1,),
        in_specs=[pl.BlockSpec((1, 3, TOK, D), lambda i: (frame, 0, 0, 0))],
        out_specs=pl.BlockSpec((HEADS, 3, HEAD_DIM, TOK), lambda i: (0, 0, 0, 0)),
        out_shape=jax.ShapeDtypeStruct((HEADS, 3, HEAD_DIM, TOK), BF16),
        compiler_params=PARAMS,
        name="pack",
    )(spatial_qkv)


def spatial_kernel(x_ref, o_ref, query, value):
    for group in range(GROUPS):
        query[group * TOK : (group + 1) * TOK, :] = x_ref[group, 0].T
        value[0:HEAD_DIM, group * TOK : (group + 1) * TOK] = x_ref[group, 2]
    value[HEAD_DIM:, :] = jnp.ones((8, GROUPS * TOK), BF16)
    keys = jnp.concatenate([x_ref[group, 1] for group in range(GROUPS)], axis=1)
    values = value[...]
    for block in range(GROUPS * TOK // QBLOCK):
        scores = matmul(query[block * QBLOCK : (block + 1) * QBLOCK, :], keys, 1, 0)
        row_max = jnp.max(scores, axis=1, keepdims=True)
        weights = jnp.exp2(scores * SCALE - row_max * SCALE).astype(BF16)
        summed = matmul(weights, values, 1, 1).T
        result = (summed[:HEAD_DIM] / summed[HEAD_DIM : HEAD_DIM + 1]).astype(BF16)
        for j in range(QBLOCK // TOK):
            o_ref[block * (QBLOCK // TOK) + j] = result[:, j * TOK : (j + 1) * TOK]


def spatial_frame(packed):
    return pl.pallas_call(
        spatial_kernel,
        in_specs=[VMEM],
        out_specs=VMEM,
        out_shape=jax.ShapeDtypeStruct((GROUPS, HEAD_DIM, TOK), BF16),
        scratch_shapes=[
            pltpu.VMEM((GROUPS * TOK, HEAD_DIM), BF16),
            pltpu.VMEM((HEAD_DIM + 8, GROUPS * TOK), BF16),
        ],
        compiler_params=PARAMS,
        name="spatial",
    )(packed)


def temporal_kernel(q_ref, kv_ref, o_ref):
    rows = PLEN * SHARE
    token_of_row = lax.broadcasted_iota(jnp.int32, (rows, rows), 0) % SHARE
    token_of_column = lax.broadcasted_iota(jnp.int32, (rows, rows), 1) % SHARE
    same_token = token_of_row == token_of_column
    queries = q_ref[...].reshape(rows, D)
    keys = kv_ref[:, 0].reshape(rows, D)
    values = kv_ref[:, 1].reshape(rows, D)
    tiles = [jnp.zeros((rows, 128), F32) for _ in range(D // 128)]
    for head in range(HEADS):
        first, last = head * HEAD_DIM // 128, ((head + 1) * HEAD_DIM - 1) // 128
        low, high = first * 128, (last + 1) * 128
        lane = lax.broadcasted_iota(jnp.int32, (rows, high - low), 1) + low
        mine = (lane >= head * HEAD_DIM) & (lane < (head + 1) * HEAD_DIM)
        q = jnp.where(mine, queries[:, low:high], 0).astype(BF16)
        v = jnp.where(mine, values[:, low:high], 0).astype(BF16)
        scores = matmul(q, keys[:, low:high], 1, 1)
        scores = jnp.where(same_token, scores * SCALE, -1e30)
        weights = jnp.exp2(scores - jnp.max(scores, axis=1, keepdims=True))
        row_sum = jnp.sum(weights, axis=1, keepdims=True)
        summed = matmul(weights.astype(BF16), v, 1, 0) / row_sum
        for tile in range(first, last + 1):
            tiles[tile] += summed[:, tile * 128 - low : tile * 128 - low + 128]
    for tile in range(D // 128):
        o_ref[:, :, tile * 128 : (tile + 1) * 128] = (
            tiles[tile].astype(BF16).reshape(PLEN, SHARE, 128)
        )


def temporal_share(query, kv):
    return pl.pallas_call(
        temporal_kernel,
        in_specs=[VMEM, VMEM],
        out_specs=VMEM,
        out_shape=jax.ShapeDtypeStruct((PLEN, SHARE, D), BF16),
        compiler_params=PARAMS,
        name="temporal",
    )(query, kv)


def combine_kernel(near_ref, far_ref, time_ref, step_ref, level_ref, gs_ref, gt_ref, table_ref, o_ref):
    for slot, space_ref in enumerate((near_ref, far_ref)):
        space = space_ref[...].astype(F32).reshape(D, TOK).T
        timely = time_ref[:, slot].astype(F32).reshape(TOK, D)
        row = step_ref[slot]
        gate_space = gs_ref[pl.ds(row, 1), :]
        gate_time = gt_ref[pl.ds(row, 1), :]
        size = table_ref[level_ref[slot]]
        o_ref[slot] = (size * (gate_space * space + gate_time * timely)).astype(BF16)


def combine(near, far, timely, steps, levels, spatial_gate, temporal_gate, step_table):
    return pl.pallas_call(
        combine_kernel,
        in_specs=[VMEM, VMEM, VMEM, SMEM, SMEM, VMEM, VMEM, SMEM],
        out_specs=VMEM,
        out_shape=jax.ShapeDtypeStruct((2, TOK, D), BF16),
        compiler_params=PARAMS,
        name="combine",
    )(near, far, timely, steps, levels, spatial_gate, temporal_gate, step_table)


def one_back(block, axes):
    size = lax.axis_size(axes)
    return lax.ppermute(block, axes, [(i, (i - 1) % size) for i in range(size)])


def exchange(block, axes):
    return lax.all_to_all(block, axes, 0, 0)


def per_device(
    spatial_qkv,
    temporal_query,
    temporal_kv,
    timestep,
    noise_level,
    spatial_gate,
    temporal_gate,
    step_table,
):
    queue = ("part", "member")
    near_in = exchange(pack_frame(spatial_qkv, 0), "sp")
    far_in = exchange(pack_frame(spatial_qkv, 1), "sp")
    ahead = one_back(jnp.stack([timestep[0], noise_level[0]]), queue)
    steps = jnp.stack([timestep[1], ahead[0]])
    levels = jnp.stack([noise_level[1], ahead[1]])
    query = temporal_query.reshape(2, 8, SHARE, D).transpose(1, 0, 2, 3)
    kv = temporal_kv.reshape(2, 2, 8, SHARE, D).transpose(2, 0, 1, 3, 4)
    query = exchange(query, "member").reshape(PLEN, SHARE, D)
    kv = exchange(kv, "member").reshape(PLEN, 2, SHARE, D)
    timely = temporal_share(query, kv)
    next_part = one_back(timely[:1], "part")
    timely = jnp.concatenate([timely[1:], next_part]).reshape(8, 2, SHARE, D)
    timely = exchange(timely, "member")
    first = exchange(spatial_frame(near_in), "sp")
    first = one_back(first, queue)
    second = exchange(spatial_frame(far_in), "sp")
    return combine(
        second, first, timely, steps, levels, spatial_gate, temporal_gate, step_table
    )


def solution(mesh):
    members = 8
    inner = Mesh(
        mesh.devices.reshape(mesh.shape["queue"] // members, members, mesh.shape["sp"]),
        ("part", "member", "sp"),
    )
    queue = ("part", "member")
    return jax.shard_map(
        per_device,
        mesh=inner,
        in_specs=(
            P(queue, None, "sp", None),
            P(queue, "sp", None),
            P(queue, None, "sp", None),
            P(queue),
            P(queue),
            P(),
            P(),
            P(),
        ),
        out_specs=P(queue, "sp", None),
        check_vma=False,
    )
```

```python
import functools
import math

import jax
import jax.numpy as jnp
from jax import lax
from jax.experimental import pallas as pl
from jax.experimental.pallas import tpu as pltpu
from jax.sharding import Mesh
from jax.sharding import PartitionSpec as P

D = 1152
HEADS = 16
HEAD_DIM = 72
PLEN = 16
GROUPS = 16
TOK = 128
QBLOCK = 256
CHIPS = 4
WIDE = 32
SHARE = 16
SCALE = math.log2(math.e) / math.sqrt(HEAD_DIM)

QUEUE = ("part", "x", "core")
F32 = jnp.float32
BF16 = jnp.bfloat16
VMEM = pl.BlockSpec(memory_space=pltpu.VMEM)
ANY = pl.BlockSpec(memory_space=pl.ANY)
SMEM = pl.BlockSpec(memory_space=pltpu.SMEM)
PARAMS = pltpu.CompilerParams(vmem_limit_bytes=56 << 20)


def matmul(a, b, a_dim, b_dim):
    return lax.dot_general(
        a, b, (((a_dim,), (b_dim,)), ((), ())), preferred_element_type=F32
    )


def resident(array):
    return pltpu.with_memory_space_constraint(array, pltpu.VMEM)


def turn(rows, write):
    turned = rows.T
    for head in range(HEADS):
        write(head, turned[head * HEAD_DIM : (head + 1) * HEAD_DIM])


def pack_kernel(parts, x_ref, time_ref, level_ref, *refs):
    o_ref, index_ref = refs[-2:]
    index_ref[0] = time_ref[0]
    index_ref[1] = level_ref[0]
    for place, (frame, part) in enumerate(parts):

        def write(head, rows, place=place):
            o_ref[head, place] = rows

        turn(x_ref[frame, part], write)


def pack(parts, spatial_qkv, timestep, noise_level, after):
    return pl.pallas_call(
        functools.partial(pack_kernel, parts),
        in_specs=[VMEM, SMEM, SMEM] + [ANY] * len(after),
        out_specs=[VMEM, SMEM],
        out_shape=[
            jax.ShapeDtypeStruct((HEADS, len(parts), HEAD_DIM, TOK), BF16),
            jax.ShapeDtypeStruct((2,), jnp.int32),
        ],
        compiler_params=PARAMS,
        name="pack",
    )(spatial_qkv, timestep, noise_level, *after)


def attend(find, query, value, write):
    for group in range(GROUPS):
        query[group * TOK : (group + 1) * TOK, :] = find(group, 0).T
        value[0:HEAD_DIM, group * TOK : (group + 1) * TOK] = find(group, 2)
    value[HEAD_DIM:, :] = jnp.ones((8, GROUPS * TOK), BF16)
    keys = jnp.concatenate([find(group, 1) for group in range(GROUPS)], axis=1)
    values = value[...]
    for block in range(GROUPS * TOK // QBLOCK):
        scores = matmul(query[block * QBLOCK : (block + 1) * QBLOCK, :], keys, 1, 0)
        row_max = jnp.max(scores, axis=1, keepdims=True)
        weights = jnp.exp2(scores * SCALE - row_max * SCALE).astype(BF16)
        summed = matmul(weights, values, 1, 1).T
        result = (summed[:HEAD_DIM] / summed[HEAD_DIM : HEAD_DIM + 1]).astype(BF16)
        for j in range(QBLOCK // TOK):
            write(block * (QBLOCK // TOK) + j, result[:, j * TOK : (j + 1) * TOK])


def first_kernel(x_ref, o_ref, query, value):
    def write(group, result):
        o_ref[group] = result

    attend(lambda group, part: x_ref[group, part], query, value, write)


def second_kernel(q_ref, kv_ref, far_ref, *refs):
    o_ref, query, value = refs[-3:]

    def find(group, part):
        return kv_ref[group, part - 1] if part else q_ref[group, 3]

    def write(group, result):
        o_ref[group, 0] = result
        o_ref[group, 1] = far_ref[group]

    attend(find, query, value, write)


SPATIAL_SCRATCH = [
    pltpu.VMEM((GROUPS * TOK, HEAD_DIM), BF16),
    pltpu.VMEM((HEAD_DIM + 8, GROUPS * TOK), BF16),
]


def first_frame(packed):
    return pl.pallas_call(
        first_kernel,
        in_specs=[VMEM],
        out_specs=VMEM,
        out_shape=jax.ShapeDtypeStruct((GROUPS, HEAD_DIM, TOK), BF16),
        scratch_shapes=SPATIAL_SCRATCH,
        compiler_params=PARAMS,
        name="first_frame",
    )(resident(packed))


def second_frame(queries, packed, far, after):
    return pl.pallas_call(
        second_kernel,
        in_specs=[VMEM, VMEM, VMEM] + [ANY] * len(after),
        out_specs=VMEM,
        out_shape=jax.ShapeDtypeStruct((GROUPS, 2, HEAD_DIM, TOK), BF16),
        scratch_shapes=SPATIAL_SCRATCH,
        compiler_params=PARAMS,
        name="second_frame",
    )(resident(queries), resident(packed), resident(far), *after)


def spread_kernel(x_ref, q_ref, kv_ref, after_ref, *o_refs):
    del after_ref
    for step, o_ref in enumerate(o_refs):
        column = lax.rem(x_ref[0] + step, CHIPS) * WIDE
        rows = pl.ds(pl.multiple_of(column, WIDE), WIDE)
        for frame in range(2):
            o_ref[frame] = q_ref[frame, rows]
            for part in range(2):
                o_ref[2 + 2 * frame + part] = kv_ref[frame, part, rows]


def spread(x, query, kv, after):
    return pl.pallas_call(
        spread_kernel,
        in_specs=[SMEM, VMEM, VMEM, ANY],
        out_specs=[VMEM] * CHIPS,
        out_shape=[jax.ShapeDtypeStruct((6, WIDE, D), BF16)] * CHIPS,
        compiler_params=PARAMS,
        name="spread",
    )(x, query, kv, after)


def swap_kernel(core_ref, *refs):
    blocks, o_ref = refs[:CHIPS], refs[CHIPS]
    half = pl.ds(pl.multiple_of((1 - core_ref[0]) * SHARE, SHARE), SHARE)
    for step in range(CHIPS):
        for row in range(6):
            o_ref[step, row] = blocks[step][row, half]


def swap_half(core, blocks):
    return pl.pallas_call(
        swap_kernel,
        in_specs=[SMEM] + [VMEM] * CHIPS,
        out_specs=VMEM,
        out_shape=jax.ShapeDtypeStruct((CHIPS, 6, SHARE, D), BF16),
        compiler_params=PARAMS,
        name="swap_half",
    )(core, *[resident(block) for block in blocks])


def temporal_kernel(core_ref, x_ref, *refs):
    blocks, other_ref = refs[:CHIPS], refs[CHIPS]
    o_ref, crossing_ref, query, key, value = refs[CHIPS + 1 :]
    half = pl.ds(pl.multiple_of(core_ref[0] * SHARE, SHARE), SHARE)
    rows = PLEN * SHARE
    token_of_row = lax.broadcasted_iota(jnp.int32, (rows, rows), 0) % SHARE
    token_of_column = lax.broadcasted_iota(jnp.int32, (rows, rows), 1) % SHARE
    same_token = token_of_row == token_of_column

    for step in range(CHIPS):
        for side in range(2):
            for frame in range(2):
                start = ((step * 2 + side) * 2 + frame) * SHARE
                place = slice(start, start + SHARE)
                for to, row in ((query, frame), (key, 2 + 2 * frame), (value, 3 + 2 * frame)):
                    to[place] = other_ref[step, row] if side else blocks[step][row, half]

    tiles = [jnp.zeros((rows, 128), F32) for _ in range(D // 128)]
    for head in range(HEADS):
        first, last = head * HEAD_DIM // 128, ((head + 1) * HEAD_DIM - 1) // 128
        low, high = first * 128, (last + 1) * 128
        lane = lax.broadcasted_iota(jnp.int32, (rows, high - low), 1) + low
        mine = (lane >= head * HEAD_DIM) & (lane < (head + 1) * HEAD_DIM)
        q = jnp.where(mine, query[:, low:high], 0).astype(BF16)
        v = jnp.where(mine, value[:, low:high], 0).astype(BF16)
        scores = matmul(q, key[:, low:high], 1, 1) * SCALE
        scores = jnp.where(same_token, scores, -1e30)
        weights = jnp.exp2(scores - jnp.max(scores, axis=1, keepdims=True))
        row_sum = jnp.sum(weights, axis=1, keepdims=True)
        summed = matmul(weights.astype(BF16), v, 1, 0) / row_sum
        for tile in range(first, last + 1):
            tiles[tile] += summed[:, tile * 128 - low : tile * 128 - low + 128]
    for step in range(CHIPS):
        for side in range(2):
            core = core_ref[0] if side == 0 else 1 - core_ref[0]
            ahead = (step + 1) % CHIPS
            even = jnp.where(core == 1, 4 * step + 1, 4 * ahead + 3)
            odd = 4 * step + 2 * core
            for frame, slot in enumerate((even, odd)):
                row = ((step * 2 + side) * 2 + frame) * SHARE
                for tile in range(D // 128):
                    o_ref[slot, :, tile * 128 : (tile + 1) * 128] = tiles[tile][
                        row : row + SHARE
                    ].astype(BF16)


    crossing_ref[...] = o_ref[crossing_slot(x_ref[0])]


def crossing_slot(x):
    return 4 * lax.rem(x + 1, CHIPS) + 3


def temporal_share(core, x, blocks, other):
    return pl.pallas_call(
        temporal_kernel,
        in_specs=[SMEM, SMEM] + [VMEM] * (CHIPS + 1),
        out_specs=[VMEM, VMEM],
        out_shape=[
            jax.ShapeDtypeStruct((PLEN, SHARE, D), BF16),
            jax.ShapeDtypeStruct((SHARE, D), BF16),
        ],
        scratch_shapes=[pltpu.VMEM((PLEN * SHARE, D), BF16)] * 3,
        compiler_params=PARAMS,
        name="temporal",
    )(core, x, *[resident(block) for block in blocks], resident(other))


def back_kernel(x_ref, timely_ref, passed_ref, *o_refs):
    slot = crossing_slot(x_ref[0])
    for step, o_ref in enumerate(o_refs):
        o_ref[...] = timely_ref[4 * step : 4 * step + 4]

        @pl.when(slot == 4 * step + 3)
        def _():
            o_ref[3] = passed_ref[...]


def to_send_back(x, timely, passed):
    return pl.pallas_call(
        back_kernel,
        in_specs=[SMEM, VMEM, VMEM],
        out_specs=[VMEM] * CHIPS,
        out_shape=[jax.ShapeDtypeStruct((4, SHARE, D), BF16)] * CHIPS,
        compiler_params=PARAMS,
        name="to_send_back",
    )(x, timely, resident(passed))


def return_kernel(core_ref, *refs):
    start = 2 * (1 - core_ref[0])
    for step in range(CHIPS):
        for slot in range(2):
            refs[CHIPS][step, slot] = refs[step][start + slot]


def return_half(core, back):
    return pl.pallas_call(
        return_kernel,
        in_specs=[SMEM] + [VMEM] * CHIPS,
        out_specs=VMEM,
        out_shape=jax.ShapeDtypeStruct((CHIPS, 2, SHARE, D), BF16),
        compiler_params=PARAMS,
        name="return_half",
    )(core, *[resident(block) for block in back])


def combine_kernel(core_ref, x_ref, space_ref, *refs):
    back, (theirs_ref, time_ref, level_ref, index_ref) = refs[:CHIPS], refs[CHIPS : CHIPS + 4]
    gs_ref, gt_ref, table_ref, o_ref, times = refs[CHIPS + 4 :]
    core = core_ref[0]
    for step in range(CHIPS):
        column = lax.rem(x_ref[0] + step, CHIPS) * WIDE
        here = pl.ds(pl.multiple_of(column + core * SHARE, SHARE), SHARE)
        there = pl.ds(pl.multiple_of(column + (1 - core) * SHARE, SHARE), SHARE)
        for slot in range(2):
            times[slot, here] = back[step][2 * core + slot]
            times[slot, there] = theirs_ref[step, slot]
    rows = time_ref[1], index_ref[0]
    levels = level_ref[1], index_ref[1]
    for slot in range(2):
        space = space_ref[:, slot].astype(F32).reshape(D, TOK).T
        timely = times[slot].astype(F32)
        gate_space = gs_ref[pl.ds(rows[slot], 1), :]
        gate_time = gt_ref[pl.ds(rows[slot], 1), :]
        size = table_ref[levels[slot]]
        o_ref[slot] = (size * (gate_space * space + gate_time * timely)).astype(BF16)


def combine(core, x, space, back, theirs, timestep, noise_level, indices, spatial_gate, temporal_gate, step_table):
    return pl.pallas_call(
        combine_kernel,
        in_specs=[SMEM, SMEM] + [VMEM] * (CHIPS + 2) + [SMEM] * 3 + [VMEM, VMEM, SMEM],
        out_specs=VMEM,
        out_shape=jax.ShapeDtypeStruct((2, TOK, D), BF16),
        scratch_shapes=[pltpu.VMEM((2, TOK, D), BF16)],
        compiler_params=PARAMS,
        name="combine",
    )(
        core, x, resident(space), *[resident(block) for block in back], resident(theirs),
        timestep, noise_level, indices, spatial_gate, temporal_gate, step_table,
    )


def shift(block, axes, distance):
    size = lax.axis_size(axes)
    return lax.ppermute(block, axes, [(i, (i + distance) % size) for i in range(size)])


def exchange(block, axes):
    return lax.all_to_all(block, axes, 0, 0)


def per_device(
    spatial_qkv,
    temporal_query,
    temporal_kv,
    timestep,
    noise_level,
    spatial_gate,
    temporal_gate,
    step_table,
):
    x, core = lax.axis_index("x"), lax.axis_index("core")
    x_arg, core_arg = x[None].astype(jnp.int32), core[None].astype(jnp.int32)
    packed, indices = pack(
        ((0, 0), (0, 1), (0, 2), (1, 0)), spatial_qkv, timestep, noise_level, ()
    )
    early = exchange(packed, "sp")
    indices = shift(indices, QUEUE, -1)
    blocks = spread(x_arg, temporal_query, temporal_kv, packed)
    blocks = [blocks[0]] + [shift(blocks[k], "x", k) for k in range(1, CHIPS)]
    packed, _ = pack(
        ((1, 1), (1, 2)), spatial_qkv, timestep, noise_level, (indices, *blocks[1:])
    )
    late = exchange(packed, "sp")
    other = shift(swap_half(core_arg, blocks), "core", 1)
    timely, passed = temporal_share(core_arg, x_arg, blocks, other)
    passed = shift(passed, "part", -1)
    back = to_send_back(x_arg, timely, passed)
    far = shift(first_frame(early), QUEUE, -1)
    space = exchange(second_frame(early, late, far, (back[0],)), "sp")
    back = [back[0]] + [shift(back[k], "x", -k) for k in range(1, CHIPS)]
    theirs = shift(return_half(core_arg, back), "core", 1)
    return combine(
        core_arg, x_arg, space, back, theirs, timestep, noise_level, indices,
        spatial_gate, temporal_gate, step_table,
    )


def solution(mesh):
    inner = Mesh(
        mesh.devices.reshape(
            mesh.shape["queue"] // (2 * CHIPS), CHIPS, 2, mesh.shape["sp"]
        ),
        QUEUE + ("sp",),
    )
    return jax.shard_map(
        per_device,
        mesh=inner,
        in_specs=(
            P(QUEUE, None, "sp", None),
            P(QUEUE, "sp", None),
            P(QUEUE, None, "sp", None),
            P(QUEUE),
            P(QUEUE),
            P(),
            P(),
            P(),
        ),
        out_specs=P(QUEUE, "sp", None),
        check_vma=False,
    )
```

```python
import functools
import math

import jax
import jax.numpy as jnp
from jax import lax
from jax.experimental import pallas as pl
from jax.experimental.pallas import tpu as pltpu
from jax.sharding import Mesh
from jax.sharding import PartitionSpec as P

D = 1152
HEADS = 16
HEAD_DIM = 72
PLEN = 16
GROUPS = 16
TOK = 128
QBLOCK = 256
CHIPS = 4
WIDE = 32
SHARE = 16
SCALE = math.log2(math.e) / math.sqrt(HEAD_DIM)

QUEUE = ("part", "x", "core")
F32 = jnp.float32
BF16 = jnp.bfloat16
VMEM = pl.BlockSpec(memory_space=pltpu.VMEM)
ANY = pl.BlockSpec(memory_space=pl.ANY)
SMEM = pl.BlockSpec(memory_space=pltpu.SMEM)
PARAMS = pltpu.CompilerParams(vmem_limit_bytes=56 << 20)


def matmul(a, b, a_dim, b_dim):
    return lax.dot_general(
        a, b, (((a_dim,), (b_dim,)), ((), ())), preferred_element_type=F32
    )


def resident(array):
    return pltpu.with_memory_space_constraint(array, pltpu.VMEM)


def turn(rows, write):
    turned = rows.T
    for head in range(HEADS):
        write(head, turned[head * HEAD_DIM : (head + 1) * HEAD_DIM])


def pack_kernel(parts, x_ref, time_ref, level_ref, *refs):
    o_ref, index_ref = refs[-2:]
    index_ref[0] = time_ref[0]
    index_ref[1] = level_ref[0]
    for place, (frame, part) in enumerate(parts):

        def write(head, rows, place=place):
            o_ref[head, place] = rows

        turn(x_ref[frame, part], write)


def pack(parts, spatial_qkv, timestep, noise_level, after):
    return pl.pallas_call(
        functools.partial(pack_kernel, parts),
        in_specs=[VMEM, SMEM, SMEM] + [ANY] * len(after),
        out_specs=[VMEM, SMEM],
        out_shape=[
            jax.ShapeDtypeStruct((HEADS, len(parts), HEAD_DIM, TOK), BF16),
            jax.ShapeDtypeStruct((2,), jnp.int32),
        ],
        compiler_params=PARAMS,
        name="pack",
    )(spatial_qkv, timestep, noise_level, *after)


def gate_kernel(*refs):
    del refs


def once_there(block, after):
    return pl.pallas_call(
        gate_kernel,
        in_specs=[ANY] * (1 + len(after)),
        out_specs=ANY,
        out_shape=jax.ShapeDtypeStruct(block.shape, block.dtype),
        input_output_aliases={0: 0},
        compiler_params=PARAMS,
        name="once_there",
    )(block, *after)


def attend(find, query, value, write):
    for group in range(GROUPS):
        query[group * TOK : (group + 1) * TOK, :] = find(group, 0).T
        value[0:HEAD_DIM, group * TOK : (group + 1) * TOK] = find(group, 2)
    value[HEAD_DIM:, :] = jnp.ones((8, GROUPS * TOK), BF16)
    keys = jnp.concatenate([find(group, 1) for group in range(GROUPS)], axis=1)
    values = value[...]
    for block in range(GROUPS * TOK // QBLOCK):
        scores = matmul(query[block * QBLOCK : (block + 1) * QBLOCK, :], keys, 1, 0)
        row_max = jnp.max(scores, axis=1, keepdims=True)
        weights = jnp.exp2(scores * SCALE - row_max * SCALE).astype(BF16)
        summed = matmul(weights, values, 1, 1).T
        result = (summed[:HEAD_DIM] / summed[HEAD_DIM : HEAD_DIM + 1]).astype(BF16)
        for j in range(QBLOCK // TOK):
            write(block * (QBLOCK // TOK) + j, result[:, j * TOK : (j + 1) * TOK])


def first_kernel(x_ref, *refs):
    o_ref, query, value = refs[-3:]

    def write(group, result):
        o_ref[group] = result

    attend(lambda group, part: x_ref[group, part], query, value, write)


def second_kernel(q_ref, kv_ref, *refs):
    o_ref, query, value = refs[-3:]

    def find(group, part):
        return kv_ref[group, part - 1] if part else q_ref[group, 3]

    def write(group, result):
        o_ref[group] = result

    attend(find, query, value, write)


SPATIAL_SCRATCH = [
    pltpu.VMEM((GROUPS * TOK, HEAD_DIM), BF16),
    pltpu.VMEM((HEAD_DIM + 8, GROUPS * TOK), BF16),
]


def first_frame(packed, after):
    return pl.pallas_call(
        first_kernel,
        in_specs=[VMEM] + [ANY] * len(after),
        out_specs=VMEM,
        out_shape=pltpu.VMEM((GROUPS, HEAD_DIM, TOK), BF16),
        scratch_shapes=SPATIAL_SCRATCH,
        compiler_params=PARAMS,
        name="first_frame",
    )(resident(packed), *after)


def second_frame(queries, packed, after):
    return pl.pallas_call(
        second_kernel,
        in_specs=[VMEM, VMEM] + [ANY] * len(after),
        out_specs=VMEM,
        out_shape=pltpu.VMEM((GROUPS, HEAD_DIM, TOK), BF16),
        scratch_shapes=SPATIAL_SCRATCH,
        compiler_params=PARAMS,
        name="second_frame",
    )(resident(queries), resident(packed), *after)


def beside_kernel(near_ref, far_ref, crossed_ref, *refs):
    o_ref = refs[-1]
    for group in range(GROUPS):
        o_ref[group, 0] = near_ref[group]
        o_ref[group, 1] = far_ref[group] + crossed_ref[group]


def beside(near, far, crossed, after):
    return pl.pallas_call(
        beside_kernel,
        in_specs=[VMEM, VMEM, VMEM] + [ANY] * len(after),
        out_specs=VMEM,
        out_shape=jax.ShapeDtypeStruct((GROUPS, 2, HEAD_DIM, TOK), BF16),
        compiler_params=PARAMS,
        name="beside",
    )(resident(near), resident(far), resident(crossed), *after)


def spread_kernel(x_ref, q_ref, kv_ref, after_ref, *o_refs):
    del after_ref
    for step, o_ref in enumerate(o_refs):
        column = lax.rem(x_ref[0] + step, CHIPS) * WIDE
        rows = pl.ds(pl.multiple_of(column, WIDE), WIDE)
        for frame in range(2):
            o_ref[frame] = q_ref[frame, rows]
            for part in range(2):
                o_ref[2 + 2 * frame + part] = kv_ref[frame, part, rows]


def spread(x, query, kv, after):
    return pl.pallas_call(
        spread_kernel,
        in_specs=[SMEM, VMEM, VMEM, ANY],
        out_specs=[VMEM] * CHIPS,
        out_shape=[jax.ShapeDtypeStruct((6, WIDE, D), BF16)] * CHIPS,
        compiler_params=PARAMS,
        name="spread",
    )(x, query, kv, after)


def swap_kernel(core_ref, *refs):
    blocks, o_ref = refs[:CHIPS], refs[CHIPS]
    half = pl.ds(pl.multiple_of((1 - core_ref[0]) * SHARE, SHARE), SHARE)
    for step in range(CHIPS):
        for row in range(6):
            o_ref[step, row] = blocks[step][row, half]


def swap_half(core, blocks):
    return pl.pallas_call(
        swap_kernel,
        in_specs=[SMEM] + [VMEM] * CHIPS,
        out_specs=VMEM,
        out_shape=jax.ShapeDtypeStruct((CHIPS, 6, SHARE, D), BF16),
        compiler_params=PARAMS,
        name="swap_half",
    )(core, *[resident(block) for block in blocks])


def temporal_kernel(core_ref, x_ref, *refs):
    blocks, other_ref = refs[:CHIPS], refs[CHIPS]
    o_ref, crossing_ref, query, key, value = refs[CHIPS + 1 :]
    half = pl.ds(pl.multiple_of(core_ref[0] * SHARE, SHARE), SHARE)
    rows = PLEN * SHARE
    token_of_row = lax.broadcasted_iota(jnp.int32, (rows, rows), 0) % SHARE
    token_of_column = lax.broadcasted_iota(jnp.int32, (rows, rows), 1) % SHARE
    same_token = token_of_row == token_of_column

    for step in range(CHIPS):
        for side in range(2):
            for frame in range(2):
                start = ((step * 2 + side) * 2 + frame) * SHARE
                place = slice(start, start + SHARE)
                for to, row in ((query, frame), (key, 2 + 2 * frame), (value, 3 + 2 * frame)):
                    to[place] = other_ref[step, row] if side else blocks[step][row, half]

    tiles = [jnp.zeros((rows, 128), F32) for _ in range(D // 128)]
    for head in range(HEADS):
        first, last = head * HEAD_DIM // 128, ((head + 1) * HEAD_DIM - 1) // 128
        low, high = first * 128, (last + 1) * 128
        lane = lax.broadcasted_iota(jnp.int32, (rows, high - low), 1) + low
        mine = (lane >= head * HEAD_DIM) & (lane < (head + 1) * HEAD_DIM)
        q = jnp.where(mine, query[:, low:high], 0).astype(BF16)
        v = jnp.where(mine, value[:, low:high], 0).astype(BF16)
        scores = matmul(q, key[:, low:high], 1, 1) * SCALE
        scores = jnp.where(same_token, scores, -1e30)
        weights = jnp.exp2(scores - jnp.max(scores, axis=1, keepdims=True))
        row_sum = jnp.sum(weights, axis=1, keepdims=True)
        summed = matmul(weights.astype(BF16), v, 1, 0) / row_sum
        for tile in range(first, last + 1):
            tiles[tile] += summed[:, tile * 128 - low : tile * 128 - low + 128]
    for step in range(CHIPS):
        for side in range(2):
            core = core_ref[0] if side == 0 else 1 - core_ref[0]
            ahead = (step + 1) % CHIPS
            even = jnp.where(core == 1, 4 * step + 1, 4 * ahead + 3)
            odd = 4 * step + 2 * core
            for frame, slot in enumerate((even, odd)):
                row = ((step * 2 + side) * 2 + frame) * SHARE
                for tile in range(D // 128):
                    o_ref[slot, :, tile * 128 : (tile + 1) * 128] = tiles[tile][
                        row : row + SHARE
                    ].astype(BF16)


    crossing_ref[...] = o_ref[crossing_slot(x_ref[0])]


def crossing_slot(x):
    return 4 * lax.rem(x + 1, CHIPS) + 3


def temporal_share(core, x, blocks, other):
    return pl.pallas_call(
        temporal_kernel,
        in_specs=[SMEM, SMEM] + [VMEM] * (CHIPS + 1),
        out_specs=[VMEM, VMEM],
        out_shape=[
            pltpu.VMEM((PLEN, SHARE, D), BF16),
            pltpu.VMEM((SHARE, D), BF16),
        ],
        scratch_shapes=[pltpu.VMEM((PLEN * SHARE, D), BF16)] * 3,
        compiler_params=PARAMS,
        name="temporal",
    )(core, x, *[resident(block) for block in blocks], resident(other))


def back_kernel(x_ref, timely_ref, passed_ref, *refs):
    o_refs = refs[-CHIPS:]
    slot = crossing_slot(x_ref[0])
    for step, o_ref in enumerate(o_refs):
        o_ref[...] = timely_ref[4 * step : 4 * step + 4]

        @pl.when(slot == 4 * step + 3)
        def _():
            o_ref[3] = passed_ref[...]


def to_send_back(x, timely, passed, after):
    return pl.pallas_call(
        back_kernel,
        in_specs=[SMEM, VMEM, VMEM] + [ANY] * len(after),
        out_specs=[VMEM] * CHIPS,
        out_shape=[pltpu.VMEM((4, SHARE, D), BF16)] * CHIPS,
        compiler_params=PARAMS,
        name="to_send_back",
    )(x, resident(timely), resident(passed), *after)


def return_kernel(core_ref, *refs):
    start = 2 * (1 - core_ref[0])
    for step in range(CHIPS):
        for slot in range(2):
            refs[CHIPS][step, slot] = refs[step][start + slot]


def return_half(core, back):
    return pl.pallas_call(
        return_kernel,
        in_specs=[SMEM] + [VMEM] * CHIPS,
        out_specs=VMEM,
        out_shape=jax.ShapeDtypeStruct((CHIPS, 2, SHARE, D), BF16),
        compiler_params=PARAMS,
        name="return_half",
    )(core, *[resident(block) for block in back])


def combine_kernel(core_ref, x_ref, space_ref, *refs):
    back, (theirs_ref, time_ref, level_ref, index_ref) = refs[:CHIPS], refs[CHIPS : CHIPS + 4]
    gs_ref, gt_ref, table_ref, o_ref, times = refs[CHIPS + 4 :]
    core = core_ref[0]
    for step in range(CHIPS):
        column = lax.rem(x_ref[0] + step, CHIPS) * WIDE
        here = pl.ds(pl.multiple_of(column + core * SHARE, SHARE), SHARE)
        there = pl.ds(pl.multiple_of(column + (1 - core) * SHARE, SHARE), SHARE)
        for slot in range(2):
            times[slot, here] = back[step][2 * core + slot]
            times[slot, there] = theirs_ref[step, slot]
    rows = time_ref[1], index_ref[0]
    levels = level_ref[1], index_ref[1]
    for slot in range(2):
        space = space_ref[:, slot].astype(F32).reshape(D, TOK).T
        timely = times[slot].astype(F32)
        gate_space = gs_ref[pl.ds(rows[slot], 1), :]
        gate_time = gt_ref[pl.ds(rows[slot], 1), :]
        size = table_ref[levels[slot]]
        o_ref[slot] = (size * (gate_space * space + gate_time * timely)).astype(BF16)


def combine(core, x, space, back, theirs, timestep, noise_level, indices, spatial_gate, temporal_gate, step_table):
    return pl.pallas_call(
        combine_kernel,
        in_specs=[SMEM, SMEM] + [VMEM] * (CHIPS + 2) + [SMEM] * 3 + [VMEM, VMEM, SMEM],
        out_specs=VMEM,
        out_shape=jax.ShapeDtypeStruct((2, TOK, D), BF16),
        scratch_shapes=[pltpu.VMEM((2, TOK, D), BF16)],
        compiler_params=PARAMS,
        name="combine",
    )(
        core, x, resident(space), *[resident(block) for block in back], resident(theirs),
        timestep, noise_level, indices, spatial_gate, temporal_gate, step_table,
    )


def shift(block, axes, distance):
    size = lax.axis_size(axes)
    return lax.ppermute(block, axes, [(i, (i + distance) % size) for i in range(size)])


def one_back(first, after):
    parts, chips, cores, groups = (lax.axis_size(a) for a in QUEUE + ("sp",))

    def number(part, x, core, group):
        return (((part % parts) * chips + x) * cores + core) * groups + group

    inside, aside, across = [], [], []
    for part in range(parts):
        for group in range(groups):
            for member in range(1, chips * cores):
                there = member - 1
                inside.append(
                    (
                        number(part, member // cores, member % cores, group),
                        number(part, there // cores, there % cores, group),
                    )
                )
            column = group * chips // groups
            between = number(part, column, 0, group)
            aside.append((number(part, 0, 0, group), between))
            across.append((between, number(part - 1, chips - 1, cores - 1, group)))
    axes = QUEUE + ("sp",)
    moved = once_there(resident(lax.ppermute(first, axes, aside)), after)
    return lax.ppermute(first, axes, inside), lax.ppermute(moved, axes, across)


def exchange(block, axes):
    return lax.all_to_all(block, axes, 0, 0)


def per_device(
    spatial_qkv,
    temporal_query,
    temporal_kv,
    timestep,
    noise_level,
    spatial_gate,
    temporal_gate,
    step_table,
):
    x, core = lax.axis_index("x"), lax.axis_index("core")
    x_arg, core_arg = x[None].astype(jnp.int32), core[None].astype(jnp.int32)
    packed, indices = pack(
        ((0, 0), (0, 1), (0, 2), (1, 0)), spatial_qkv, timestep, noise_level, ()
    )
    early = exchange(packed, "sp")
    indices = shift(indices, QUEUE, -1)
    blocks = spread(x_arg, temporal_query, temporal_kv, packed)
    packed, _ = pack(
        ((1, 1), (1, 2)), spatial_qkv, timestep, noise_level, blocks[:1]
    )
    blocks = [blocks[0]] + [shift(blocks[k], "x", k) for k in range(1, CHIPS)]
    half = swap_half(core_arg, blocks)
    late = exchange(once_there(packed, (indices, half)), "sp")
    other = shift(half, "core", 1)
    timely, passed = temporal_share(core_arg, x_arg, blocks, other)
    passed = shift(passed, "part", -1)
    first = first_frame(early, ())
    far, crossed = one_back(first, (resident(timely),))
    near = second_frame(early, late, (resident(timely),))
    back = to_send_back(x_arg, timely, passed, (resident(near),))
    space = exchange(beside(near, far, crossed, (resident(back[0]),)), "sp")
    back = [back[0]] + [shift(back[k], "x", -k) for k in range(1, CHIPS)]
    theirs = shift(return_half(core_arg, back), "core", 1)
    return combine(
        core_arg, x_arg, space, back, theirs, timestep, noise_level, indices,
        spatial_gate, temporal_gate, step_table,
    )


def solution(mesh):
    inner = Mesh(
        mesh.devices.reshape(
            mesh.shape["queue"] // (2 * CHIPS), CHIPS, 2, mesh.shape["sp"]
        ),
        QUEUE + ("sp",),
    )
    return jax.shard_map(
        per_device,
        mesh=inner,
        in_specs=(
            P(QUEUE, None, "sp", None),
            P(QUEUE, "sp", None),
            P(QUEUE, None, "sp", None),
            P(QUEUE),
            P(QUEUE),
            P(),
            P(),
            P(),
        ),
        out_specs=P(QUEUE, "sp", None),
        check_vma=False,
    )
```

```python
import functools
import math

import jax
import jax.numpy as jnp
from jax import lax
from jax.experimental import pallas as pl
from jax.experimental.pallas import tpu as pltpu
from jax.sharding import Mesh
from jax.sharding import PartitionSpec as P

D = 1152
HEADS = 16
HEAD_DIM = 72
PLEN = 16
GROUPS = 16
TOK = 128
QBLOCK = 256
CHIPS = 4
MEMBERS = 8
WIDE = 32
SHARE = 16
SCALE = math.log2(math.e) / math.sqrt(HEAD_DIM)

QUEUE = ("part", "x", "core")
F32 = jnp.float32
BF16 = jnp.bfloat16
VMEM = pl.BlockSpec(memory_space=pltpu.VMEM)
ANY = pl.BlockSpec(memory_space=pl.ANY)
SMEM = pl.BlockSpec(memory_space=pltpu.SMEM)
PARAMS = pltpu.CompilerParams(vmem_limit_bytes=16 << 20)
WIDE_PARAMS = pltpu.CompilerParams(vmem_limit_bytes=32 << 20)


def matmul(a, b, a_dim, b_dim):
    return lax.dot_general(
        a, b, (((a_dim,), (b_dim,)), ((), ())), preferred_element_type=F32
    )


def outside(array):
    return pltpu.with_memory_space_constraint(array, pltpu.HBM)


def resident(array):
    return pltpu.with_memory_space_constraint(array, pltpu.VMEM)


def turn(rows, write):
    turned = rows.T
    for head in range(HEADS):
        write(head, turned[head * HEAD_DIM : (head + 1) * HEAD_DIM])


def pack_kernel(x_ref, time_ref, level_ref, *refs):
    o_ref, index_ref = refs[-2:]
    index_ref[0] = time_ref[0]
    index_ref[1] = level_ref[0]

    def write(head, rows):
        o_ref[head, 0] = rows

    turn(x_ref[0, 0], write)


def pack(frame, spatial_qkv, timestep, noise_level, after):
    return pl.pallas_call(
        pack_kernel,
        grid=(3,),
        in_specs=[pl.BlockSpec((1, 1, TOK, D), lambda part: (frame, part, 0, 0)), SMEM, SMEM]
        + [ANY] * len(after),
        out_specs=[
            pl.BlockSpec((HEADS, 1, HEAD_DIM, TOK), lambda part: (0, part, 0, 0)),
            SMEM,
        ],
        out_shape=[
            jax.ShapeDtypeStruct((HEADS, 3, HEAD_DIM, TOK), BF16),
            jax.ShapeDtypeStruct((2,), jnp.int32),
        ],
        compiler_params=PARAMS,
        name="pack",
    )(outside(spatial_qkv), timestep, noise_level, *after)


def gate_kernel(*refs):
    del refs


def once_there(block, after):
    return pl.pallas_call(
        gate_kernel,
        in_specs=[ANY] * (1 + len(after)),
        out_specs=ANY,
        out_shape=jax.ShapeDtypeStruct(block.shape, block.dtype),
        input_output_aliases={0: 0},
        compiler_params=PARAMS,
        name="once_there",
    )(block, *after)


def attend(find, query, value, write):
    for group in range(GROUPS):
        query[group * TOK : (group + 1) * TOK, :] = find(group, 0).T
        value[0:HEAD_DIM, group * TOK : (group + 1) * TOK] = find(group, 2)
    value[HEAD_DIM:, :] = jnp.ones((8, GROUPS * TOK), BF16)
    keys = jnp.concatenate([find(group, 1) for group in range(GROUPS)], axis=1)
    values = value[...]
    for block in range(GROUPS * TOK // QBLOCK):
        scores = matmul(query[block * QBLOCK : (block + 1) * QBLOCK, :], keys, 1, 0)
        row_max = jnp.max(scores, axis=1, keepdims=True)
        weights = jnp.exp2(scores * SCALE - row_max * SCALE).astype(BF16)
        summed = matmul(weights, values, 1, 1).T
        result = (summed[:HEAD_DIM] / summed[HEAD_DIM : HEAD_DIM + 1]).astype(BF16)
        for j in range(QBLOCK // TOK):
            write(block * (QBLOCK // TOK) + j, result[:, j * TOK : (j + 1) * TOK])


def spatial_kernel(x_ref, *refs):
    o_ref, query, value = refs[-3:]

    def write(group, result):
        o_ref[group] = result

    attend(lambda group, part: x_ref[group, part], query, value, write)


SPATIAL_SCRATCH = [
    pltpu.VMEM((GROUPS * TOK, HEAD_DIM), BF16),
    pltpu.VMEM((HEAD_DIM + 8, GROUPS * TOK), BF16),
]


def spatial_frame(packed, after):
    return pl.pallas_call(
        spatial_kernel,
        in_specs=[VMEM] + [ANY] * len(after),
        out_specs=VMEM,
        out_shape=pltpu.VMEM((GROUPS, HEAD_DIM, TOK), BF16),
        scratch_shapes=SPATIAL_SCRATCH,
        compiler_params=WIDE_PARAMS,
        name="spatial",
    )(resident(packed), *after)


def beside_kernel(near_ref, far_ref, crossed_ref, *refs):
    o_ref = refs[-1]
    for group in range(GROUPS):
        o_ref[group, 0] = near_ref[group]
        o_ref[group, 1] = far_ref[group] + crossed_ref[group]


def beside(near, far, crossed, after):
    return pl.pallas_call(
        beside_kernel,
        in_specs=[VMEM, VMEM, VMEM] + [ANY] * len(after),
        out_specs=VMEM,
        out_shape=jax.ShapeDtypeStruct((GROUPS, 2, HEAD_DIM, TOK), BF16),
        compiler_params=PARAMS,
        name="beside",
    )(resident(near), resident(far), resident(crossed), *after)


def spread_kernel(x_ref, q_ref, kv_ref, after_ref, *o_refs):
    del after_ref
    for step, o_ref in enumerate(o_refs):
        column = lax.rem(x_ref[0] + step, CHIPS) * WIDE
        rows = pl.ds(pl.multiple_of(column, WIDE), WIDE)
        for frame in range(2):
            o_ref[frame] = q_ref[frame, rows]
            for part in range(2):
                o_ref[2 + 2 * frame + part] = kv_ref[frame, part, rows]


def spread(x, query, kv, after):
    return pl.pallas_call(
        spread_kernel,
        in_specs=[SMEM, VMEM, VMEM, ANY],
        out_specs=[VMEM] * CHIPS,
        out_shape=[jax.ShapeDtypeStruct((6, WIDE, D), BF16)] * CHIPS,
        compiler_params=PARAMS,
        name="spread",
    )(x, outside(query), outside(kv), after)


def swap_kernel(core_ref, *refs):
    blocks, o_ref = refs[:CHIPS], refs[-1]
    half = pl.ds(pl.multiple_of((1 - core_ref[0]) * SHARE, SHARE), SHARE)
    for step in range(CHIPS):
        for row in range(6):
            o_ref[step, row] = blocks[step][row, half]


def swap_half(core, blocks, after):
    return pl.pallas_call(
        swap_kernel,
        in_specs=[SMEM] + [VMEM] * CHIPS + [ANY] * len(after),
        out_specs=VMEM,
        out_shape=jax.ShapeDtypeStruct((CHIPS, 6, SHARE, D), BF16),
        compiler_params=PARAMS,
        name="swap_half",
    )(core, *[resident(block) for block in blocks], *after)


def temporal_kernel(core_ref, *refs):
    blocks, other_ref = refs[:CHIPS], refs[CHIPS]
    mine_ref, send_ref, query, key, value = refs[CHIPS + 1 :]
    half = pl.ds(pl.multiple_of(core_ref[0] * SHARE, SHARE), SHARE)
    rows = PLEN * SHARE
    token_of_row = lax.broadcasted_iota(jnp.int32, (rows, rows), 0) % SHARE
    token_of_column = lax.broadcasted_iota(jnp.int32, (rows, rows), 1) % SHARE
    same_token = token_of_row == token_of_column

    for step in range(CHIPS):
        for side in range(2):
            for frame in range(2):
                start = ((step * 2 + side) * 2 + frame) * SHARE
                place = slice(start, start + SHARE)
                for to, row in ((query, frame), (key, 2 + 2 * frame), (value, 3 + 2 * frame)):
                    to[place] = other_ref[step, row] if side else blocks[step][row, half]

    tiles = [jnp.zeros((rows, 128), F32) for _ in range(D // 128)]
    for head in range(HEADS):
        first, last = head * HEAD_DIM // 128, ((head + 1) * HEAD_DIM - 1) // 128
        low, high = first * 128, (last + 1) * 128
        lane = lax.broadcasted_iota(jnp.int32, (rows, high - low), 1) + low
        mine = (lane >= head * HEAD_DIM) & (lane < (head + 1) * HEAD_DIM)
        q = jnp.where(mine, query[:, low:high], 0).astype(BF16)
        v = jnp.where(mine, value[:, low:high], 0).astype(BF16)
        scores = matmul(q, key[:, low:high], 1, 1) * SCALE
        scores = jnp.where(same_token, scores, -1e30)
        weights = jnp.exp2(scores - jnp.max(scores, axis=1, keepdims=True))
        row_sum = jnp.sum(weights, axis=1, keepdims=True)
        summed = matmul(weights.astype(BF16), v, 1, 0) / row_sum
        for tile in range(first, last + 1):
            tiles[tile] += summed[:, tile * 128 - low : tile * 128 - low + 128]
    core = core_ref[0]
    for step in range(CHIPS):
        for side, (odd_ref, even_ref, ahead) in enumerate(
            ((mine_ref, send_ref, 1 - core), (send_ref, mine_ref, core))
        ):
            back = lax.rem(step + ahead, CHIPS)
            for frame, (ref, place) in enumerate(
                ((even_ref, 2 * back + 1), (odd_ref, 2 * step))
            ):
                row = ((step * 2 + side) * 2 + frame) * SHARE
                for tile in range(D // 128):
                    ref[place, :, tile * 128 : (tile + 1) * 128] = tiles[tile][
                        row : row + SHARE
                    ].astype(BF16)


def temporal_share(core, blocks, other):
    return pl.pallas_call(
        temporal_kernel,
        in_specs=[SMEM] + [VMEM] * (CHIPS + 1),
        out_specs=[VMEM, VMEM],
        out_shape=[pltpu.VMEM((2 * CHIPS, SHARE, D), BF16)] * 2,
        scratch_shapes=[pltpu.VMEM((PLEN * SHARE, D), BF16)] * 3,
        compiler_params=PARAMS,
        name="temporal",
    )(core, *[resident(block) for block in blocks], resident(other))


def edge_kernel(x_ref, mine_ref, theirs_ref, o_ref):
    slot = 2 * lax.rem(x_ref[0] + 1, CHIPS) + 1
    o_ref[0] = mine_ref[slot]
    o_ref[1] = theirs_ref[slot]


def edge(x, mine, theirs):
    return pl.pallas_call(
        edge_kernel,
        in_specs=[SMEM, VMEM, VMEM],
        out_specs=VMEM,
        out_shape=pltpu.VMEM((2, SHARE, D), BF16),
        compiler_params=PARAMS,
        name="edge",
    )(x, resident(mine), resident(theirs))


def back_kernel(core_ref, x_ref, mine_ref, theirs_ref, passed_ref, *refs):
    slot = 2 * lax.rem(x_ref[0] + 1, CHIPS) + 1
    for step, o_ref in enumerate(refs[-CHIPS:]):
        o_ref[0:2] = mine_ref[2 * step : 2 * step + 2]
        o_ref[2:4] = theirs_ref[2 * step : 2 * step + 2]

        @pl.when((slot == 2 * step + 1) & (core_ref[0] == 1))
        def _(o_ref=o_ref):
            o_ref[1] = passed_ref[0]
            o_ref[3] = passed_ref[1]


def to_send_back(core, x, mine, theirs, passed, after):
    return pl.pallas_call(
        back_kernel,
        in_specs=[SMEM, SMEM, VMEM, VMEM, VMEM] + [ANY] * len(after),
        out_specs=[VMEM] * CHIPS,
        out_shape=[pltpu.VMEM((4, SHARE, D), BF16)] * CHIPS,
        compiler_params=PARAMS,
        name="to_send_back",
    )(core, x, resident(mine), resident(theirs), resident(passed), *after)


def combine_kernel(core_ref, x_ref, space_ref, *refs):
    back, (time_ref, level_ref, index_ref) = refs[:CHIPS], refs[CHIPS : CHIPS + 3]
    gs_ref, gt_ref, table_ref, o_ref, times = refs[CHIPS + 3 :]
    core = core_ref[0]
    for step in range(CHIPS):
        column = lax.rem(x_ref[0] + step, CHIPS) * WIDE
        here = pl.ds(pl.multiple_of(column + core * SHARE, SHARE), SHARE)
        there = pl.ds(pl.multiple_of(column + (1 - core) * SHARE, SHARE), SHARE)
        for slot in range(2):
            times[slot, here] = back[step][slot]
            times[slot, there] = back[step][2 + slot]
    rows = time_ref[1], index_ref[0]
    levels = level_ref[1], index_ref[1]
    for slot in range(2):
        space = space_ref[:, slot].astype(F32).reshape(D, TOK).T
        timely = times[slot].astype(F32)
        gate_space = gs_ref[pl.ds(rows[slot], 1), :]
        gate_time = gt_ref[pl.ds(rows[slot], 1), :]
        size = table_ref[levels[slot]]
        o_ref[slot] = (size * (gate_space * space + gate_time * timely)).astype(BF16)


def combine(core, x, space, back, timestep, noise_level, indices, spatial_gate, temporal_gate, step_table):
    return pl.pallas_call(
        combine_kernel,
        in_specs=[SMEM, SMEM] + [VMEM] * (CHIPS + 1) + [SMEM] * 3 + [VMEM, VMEM, SMEM],
        out_specs=VMEM,
        out_shape=jax.ShapeDtypeStruct((2, TOK, D), BF16),
        scratch_shapes=[pltpu.VMEM((2, TOK, D), BF16)],
        compiler_params=PARAMS,
        name="combine",
    )(
        core, x, resident(space), *[resident(block) for block in back],
        timestep, noise_level, indices, spatial_gate, temporal_gate, step_table,
    )


def shift(block, axes, distance):
    size = lax.axis_size(axes)
    return lax.ppermute(block, axes, [(i, (i + distance) % size) for i in range(size)])


def one_back(first, after):
    parts, chips, cores, groups = (lax.axis_size(a) for a in QUEUE + ("sp",))

    def number(part, x, core, group):
        return (((part % parts) * chips + x) * cores + core) * groups + group

    inside, aside, across = [], [], []
    for part in range(parts):
        for group in range(groups):
            for member in range(1, chips * cores):
                there = member - 1
                inside.append(
                    (
                        number(part, member // cores, member % cores, group),
                        number(part, there // cores, there % cores, group),
                    )
                )
            column = group * chips // groups
            between = number(part, column, 0, group)
            aside.append((number(part, 0, 0, group), between))
            across.append((between, number(part - 1, chips - 1, cores - 1, group)))
    axes = QUEUE + ("sp",)
    moved = once_there(resident(lax.ppermute(first, axes, aside)), after)
    return lax.ppermute(first, axes, inside), lax.ppermute(moved, axes, across)


def exchange(block, axes):
    return lax.all_to_all(block, axes, 0, 0)


def per_device(
    spatial_qkv,
    temporal_query,
    temporal_kv,
    timestep,
    noise_level,
    spatial_gate,
    temporal_gate,
    step_table,
):
    x, core = lax.axis_index("x"), lax.axis_index("core")
    x_arg, core_arg = x[None].astype(jnp.int32), core[None].astype(jnp.int32)
    packed, indices = pack(0, spatial_qkv, timestep, noise_level, ())
    early = exchange(packed, "sp")
    indices = shift(indices, QUEUE, -1)
    blocks = spread(x_arg, temporal_query, temporal_kv, packed)
    packed, _ = pack(1, spatial_qkv, timestep, noise_level, blocks[:1])
    moved = {k: shift(blocks[k], "x", k) for k in (2, 3, 1)}
    blocks = [blocks[0]] + [moved[k] for k in range(1, CHIPS)]
    first = spatial_frame(early, ())
    half = swap_half(core_arg, blocks, (resident(first),))
    late = exchange(once_there(packed, (indices, half)), "sp")
    other = shift(half, "core", 1)
    mine, send = temporal_share(core_arg, blocks, other)
    theirs = shift(send, "core", 1)
    size = lax.axis_size(QUEUE)
    passed = lax.ppermute(
        edge(x_arg, mine, theirs),
        QUEUE,
        [(i, (i - MEMBERS) % size) for i in range(1, size, 2)],
    )
    far, crossed = one_back(first, (resident(mine),))
    near = spatial_frame(late, (resident(mine),))
    back = to_send_back(core_arg, x_arg, mine, theirs, passed, (resident(near),))
    space = exchange(beside(near, far, crossed, (resident(back[0]),)), "sp")
    back = [back[0]] + [shift(back[k], "x", -k) for k in range(1, CHIPS)]
    return combine(
        core_arg, x_arg, space, back, timestep, noise_level, indices,
        spatial_gate, temporal_gate, step_table,
    )


def solution(mesh):
    inner = Mesh(
        mesh.devices.reshape(
            mesh.shape["queue"] // (2 * CHIPS), CHIPS, 2, mesh.shape["sp"]
        ),
        QUEUE + ("sp",),
    )
    return jax.shard_map(
        per_device,
        mesh=inner,
        in_specs=(
            P(QUEUE, None, "sp", None),
            P(QUEUE, "sp", None),
            P(QUEUE, None, "sp", None),
            P(QUEUE),
            P(QUEUE),
            P(),
            P(),
            P(),
        ),
        out_specs=P(QUEUE, "sp", None),
        check_vma=False,
    )
```

```python
import functools
import math

import jax
import jax.numpy as jnp
from jax import lax
from jax.experimental import pallas as pl
from jax.experimental.pallas import tpu as pltpu
from jax.sharding import Mesh
from jax.sharding import PartitionSpec as P

D = 1152
HEADS = 16
HEAD_DIM = 72
PLEN = 16
GROUPS = 16
TOK = 128
QBLOCK = 256
CHIPS = 4
MEMBERS = 8
WIDE = 32
SHARE = 16
SCALE = math.log2(math.e) / math.sqrt(HEAD_DIM)

QUEUE = ("part", "x", "core")
F32 = jnp.float32
BF16 = jnp.bfloat16
VMEM = pl.BlockSpec(memory_space=pltpu.VMEM)
ANY = pl.BlockSpec(memory_space=pl.ANY)
SMEM = pl.BlockSpec(memory_space=pltpu.SMEM)
PARAMS = pltpu.CompilerParams(vmem_limit_bytes=16 << 20)
WIDE_PARAMS = pltpu.CompilerParams(vmem_limit_bytes=32 << 20)


def matmul(a, b, a_dim, b_dim):
    return lax.dot_general(
        a, b, (((a_dim,), (b_dim,)), ((), ())), preferred_element_type=F32
    )


def outside(array):
    return pltpu.with_memory_space_constraint(array, pltpu.HBM)


def resident(array):
    return pltpu.with_memory_space_constraint(array, pltpu.VMEM)


def turn(rows, write):
    turned = rows.T
    for head in range(HEADS):
        write(head, turned[head * HEAD_DIM : (head + 1) * HEAD_DIM])


def pack_kernel(x_ref, time_ref, level_ref, *refs):
    o_ref, index_ref = refs[-2:]
    index_ref[0] = time_ref[0]
    index_ref[1] = level_ref[0]

    def write(head, rows):
        o_ref[head, 0] = rows

    turn(x_ref[0, 0], write)


def pack(frame, spatial_qkv, timestep, noise_level, after):
    return pl.pallas_call(
        pack_kernel,
        grid=(3,),
        in_specs=[pl.BlockSpec((1, 1, TOK, D), lambda part: (frame, part, 0, 0)), SMEM, SMEM]
        + [ANY] * len(after),
        out_specs=[
            pl.BlockSpec((HEADS, 1, HEAD_DIM, TOK), lambda part: (0, part, 0, 0)),
            SMEM,
        ],
        out_shape=[
            jax.ShapeDtypeStruct((HEADS, 3, HEAD_DIM, TOK), BF16),
            jax.ShapeDtypeStruct((2,), jnp.int32),
        ],
        compiler_params=PARAMS,
        name="pack",
    )(outside(spatial_qkv), timestep, noise_level, *after)


def gate_kernel(*refs):
    del refs


def once_there(block, after):
    return pl.pallas_call(
        gate_kernel,
        in_specs=[ANY] * (1 + len(after)),
        out_specs=ANY,
        out_shape=jax.ShapeDtypeStruct(block.shape, block.dtype),
        input_output_aliases={0: 0},
        compiler_params=PARAMS,
        name="once_there",
    )(block, *after)


def attend(find, query, value, write):
    for group in range(GROUPS):
        query[group * TOK : (group + 1) * TOK, :] = find(group, 0).T
        value[0:HEAD_DIM, group * TOK : (group + 1) * TOK] = find(group, 2)
    value[HEAD_DIM:, :] = jnp.ones((8, GROUPS * TOK), BF16)
    keys = jnp.concatenate([find(group, 1) for group in range(GROUPS)], axis=1)
    values = value[...]
    for block in range(GROUPS * TOK // QBLOCK):
        scores = matmul(query[block * QBLOCK : (block + 1) * QBLOCK, :], keys, 1, 0)
        row_max = jnp.max(scores, axis=1, keepdims=True)
        weights = jnp.exp2(scores * SCALE - row_max * SCALE).astype(BF16)
        summed = matmul(weights, values, 1, 1).T
        result = (summed[:HEAD_DIM] / summed[HEAD_DIM : HEAD_DIM + 1]).astype(BF16)
        for j in range(QBLOCK // TOK):
            write(block * (QBLOCK // TOK) + j, result[:, j * TOK : (j + 1) * TOK])


def spatial_kernel(x_ref, *refs):
    o_ref, query, value = refs[-3:]

    def write(group, result):
        o_ref[group] = result

    attend(lambda group, part: x_ref[group, part], query, value, write)


SPATIAL_SCRATCH = [
    pltpu.VMEM((GROUPS * TOK, HEAD_DIM), BF16),
    pltpu.VMEM((HEAD_DIM + 8, GROUPS * TOK), BF16),
]


def spatial_frame(packed, after):
    return pl.pallas_call(
        spatial_kernel,
        in_specs=[VMEM] + [ANY] * len(after),
        out_specs=VMEM,
        out_shape=pltpu.VMEM((GROUPS, HEAD_DIM, TOK), BF16),
        scratch_shapes=SPATIAL_SCRATCH,
        compiler_params=WIDE_PARAMS,
        name="spatial",
    )(resident(packed), *after)


def beside_kernel(near_ref, far_ref, crossed_ref, *refs):
    o_ref = refs[-1]
    for group in range(GROUPS):
        o_ref[group, 0] = near_ref[group]
        o_ref[group, 1] = far_ref[group] + crossed_ref[group]


def beside(near, far, crossed, after):
    return pl.pallas_call(
        beside_kernel,
        in_specs=[VMEM, VMEM, VMEM] + [ANY] * len(after),
        out_specs=VMEM,
        out_shape=jax.ShapeDtypeStruct((GROUPS, 2, HEAD_DIM, TOK), BF16),
        compiler_params=PARAMS,
        name="beside",
    )(resident(near), resident(far), resident(crossed), *after)


def piece(refs, step, row):
    if step == 2:
        return refs[2 + row // 3], row % 3
    return refs[step + (step > 2)], row


def put(refs, step, row, tokens):
    ref, place = piece(refs, step, row)
    ref[place] = tokens


def spread_kernel(x_ref, q_ref, kv_ref, after_ref, *o_refs):
    del after_ref
    for step in range(CHIPS):
        column = lax.rem(x_ref[0] + step, CHIPS) * WIDE
        rows = pl.ds(pl.multiple_of(column, WIDE), WIDE)
        for frame in range(2):
            put(o_refs, step, frame, q_ref[frame, rows])
            for part in range(2):
                put(o_refs, step, 2 + 2 * frame + part, kv_ref[frame, part, rows])


def spread(x, query, kv, after):
    return pl.pallas_call(
        spread_kernel,
        in_specs=[SMEM, VMEM, VMEM, ANY],
        out_specs=[VMEM] * (CHIPS + 1),
        out_shape=[
            jax.ShapeDtypeStruct((rows, WIDE, D), BF16) for rows in (6, 6, 3, 3, 6)
        ],
        compiler_params=PARAMS,
        name="spread",
    )(x, outside(query), outside(kv), after)


def swap_kernel(core_ref, *refs):
    blocks, o_ref = refs[: CHIPS + 1], refs[-1]
    half = pl.ds(pl.multiple_of((1 - core_ref[0]) * SHARE, SHARE), SHARE)
    for step in range(CHIPS):
        for row in range(6):
            ref, place = piece(blocks, step, row)
            o_ref[step, row] = ref[place, half]


def swap_half(core, blocks, after):
    return pl.pallas_call(
        swap_kernel,
        in_specs=[SMEM] + [VMEM] * (CHIPS + 1) + [ANY] * len(after),
        out_specs=VMEM,
        out_shape=jax.ShapeDtypeStruct((CHIPS, 6, SHARE, D), BF16),
        compiler_params=PARAMS,
        name="swap_half",
    )(core, *[resident(block) for block in blocks], *after)


def temporal_kernel(core_ref, *refs):
    blocks, other_ref = refs[: CHIPS + 1], refs[CHIPS + 1]
    mine_ref, send_ref, query, key, value = refs[CHIPS + 2 :]
    half = pl.ds(pl.multiple_of(core_ref[0] * SHARE, SHARE), SHARE)
    rows = PLEN * SHARE
    token_of_row = lax.broadcasted_iota(jnp.int32, (rows, rows), 0) % SHARE
    token_of_column = lax.broadcasted_iota(jnp.int32, (rows, rows), 1) % SHARE
    same_token = token_of_row == token_of_column

    for step in range(CHIPS):
        for side in range(2):
            for frame in range(2):
                start = ((step * 2 + side) * 2 + frame) * SHARE
                place = slice(start, start + SHARE)
                for to, row in ((query, frame), (key, 2 + 2 * frame), (value, 3 + 2 * frame)):
                    ref, found = piece(blocks, step, row)
                    to[place] = other_ref[step, row] if side else ref[found, half]

    tiles = [jnp.zeros((rows, 128), F32) for _ in range(D // 128)]
    for head in range(HEADS):
        first, last = head * HEAD_DIM // 128, ((head + 1) * HEAD_DIM - 1) // 128
        low, high = first * 128, (last + 1) * 128
        lane = lax.broadcasted_iota(jnp.int32, (rows, high - low), 1) + low
        mine = (lane >= head * HEAD_DIM) & (lane < (head + 1) * HEAD_DIM)
        q = jnp.where(mine, query[:, low:high], 0).astype(BF16)
        v = jnp.where(mine, value[:, low:high], 0).astype(BF16)
        scores = matmul(q, key[:, low:high], 1, 1) * SCALE
        scores = jnp.where(same_token, scores, -1e30)
        weights = jnp.exp2(scores - jnp.max(scores, axis=1, keepdims=True))
        row_sum = jnp.sum(weights, axis=1, keepdims=True)
        summed = matmul(weights.astype(BF16), v, 1, 0) / row_sum
        for tile in range(first, last + 1):
            tiles[tile] += summed[:, tile * 128 - low : tile * 128 - low + 128]
    core = core_ref[0]
    for step in range(CHIPS):
        for side, (odd_ref, even_ref, ahead) in enumerate(
            ((mine_ref, send_ref, 1 - core), (send_ref, mine_ref, core))
        ):
            back = lax.rem(step + ahead, CHIPS)
            for frame, (ref, place) in enumerate(
                ((even_ref, 2 * back + 1), (odd_ref, 2 * step))
            ):
                row = ((step * 2 + side) * 2 + frame) * SHARE
                for tile in range(D // 128):
                    ref[place, :, tile * 128 : (tile + 1) * 128] = tiles[tile][
                        row : row + SHARE
                    ].astype(BF16)


def temporal_share(core, blocks, other):
    return pl.pallas_call(
        temporal_kernel,
        in_specs=[SMEM] + [VMEM] * (CHIPS + 2),
        out_specs=[VMEM, VMEM],
        out_shape=[pltpu.VMEM((2 * CHIPS, SHARE, D), BF16)] * 2,
        scratch_shapes=[pltpu.VMEM((PLEN * SHARE, D), BF16)] * 3,
        compiler_params=PARAMS,
        name="temporal",
    )(core, *[resident(block) for block in blocks], resident(other))


def edge_kernel(x_ref, mine_ref, theirs_ref, o_ref):
    slot = 2 * lax.rem(x_ref[0] + 1, CHIPS) + 1
    o_ref[0] = mine_ref[slot]
    o_ref[1] = theirs_ref[slot]


def edge(x, mine, theirs):
    return pl.pallas_call(
        edge_kernel,
        in_specs=[SMEM, VMEM, VMEM],
        out_specs=VMEM,
        out_shape=pltpu.VMEM((2, SHARE, D), BF16),
        compiler_params=PARAMS,
        name="edge",
    )(x, resident(mine), resident(theirs))


def back_kernel(core_ref, x_ref, mine_ref, theirs_ref, passed_ref, *refs):
    slot = 2 * lax.rem(x_ref[0] + 1, CHIPS) + 1
    for step, o_ref in enumerate(refs[-CHIPS:]):
        o_ref[0:2] = mine_ref[2 * step : 2 * step + 2]
        o_ref[2:4] = theirs_ref[2 * step : 2 * step + 2]

        @pl.when((slot == 2 * step + 1) & (core_ref[0] == 1))
        def _(o_ref=o_ref):
            o_ref[1] = passed_ref[0]
            o_ref[3] = passed_ref[1]


def to_send_back(core, x, mine, theirs, passed, after):
    return pl.pallas_call(
        back_kernel,
        in_specs=[SMEM, SMEM, VMEM, VMEM, VMEM] + [ANY] * len(after),
        out_specs=[VMEM] * CHIPS,
        out_shape=[pltpu.VMEM((4, SHARE, D), BF16)] * CHIPS,
        compiler_params=PARAMS,
        name="to_send_back",
    )(core, x, resident(mine), resident(theirs), resident(passed), *after)


def combine_kernel(core_ref, x_ref, space_ref, *refs):
    back, (time_ref, level_ref, index_ref) = refs[:CHIPS], refs[CHIPS : CHIPS + 3]
    gs_ref, gt_ref, table_ref, o_ref, times = refs[CHIPS + 3 :]
    core = core_ref[0]
    for step in range(CHIPS):
        column = lax.rem(x_ref[0] + step, CHIPS) * WIDE
        here = pl.ds(pl.multiple_of(column + core * SHARE, SHARE), SHARE)
        there = pl.ds(pl.multiple_of(column + (1 - core) * SHARE, SHARE), SHARE)
        for slot in range(2):
            times[slot, here] = back[step][slot]
            times[slot, there] = back[step][2 + slot]
    rows = time_ref[1], index_ref[0]
    levels = level_ref[1], index_ref[1]
    for slot in range(2):
        space = space_ref[:, slot].astype(F32).reshape(D, TOK).T
        timely = times[slot].astype(F32)
        gate_space = gs_ref[pl.ds(rows[slot], 1), :]
        gate_time = gt_ref[pl.ds(rows[slot], 1), :]
        size = table_ref[levels[slot]]
        o_ref[slot] = (size * (gate_space * space + gate_time * timely)).astype(BF16)


def combine(core, x, space, back, timestep, noise_level, indices, spatial_gate, temporal_gate, step_table):
    return pl.pallas_call(
        combine_kernel,
        in_specs=[SMEM, SMEM] + [VMEM] * (CHIPS + 1) + [SMEM] * 3 + [VMEM, VMEM, SMEM],
        out_specs=VMEM,
        out_shape=jax.ShapeDtypeStruct((2, TOK, D), BF16),
        scratch_shapes=[pltpu.VMEM((2, TOK, D), BF16)],
        compiler_params=PARAMS,
        name="combine",
    )(
        core, x, resident(space), *[resident(block) for block in back],
        timestep, noise_level, indices, spatial_gate, temporal_gate, step_table,
    )


def shift(block, axes, distance):
    size = lax.axis_size(axes)
    return lax.ppermute(block, axes, [(i, (i + distance) % size) for i in range(size)])


def one_back(first, after):
    parts, chips, cores, groups = (lax.axis_size(a) for a in QUEUE + ("sp",))

    def number(part, x, core, group):
        return (((part % parts) * chips + x) * cores + core) * groups + group

    inside, aside, across = [], [], []
    for part in range(parts):
        for group in range(groups):
            for member in range(1, chips * cores):
                there = member - 1
                inside.append(
                    (
                        number(part, member // cores, member % cores, group),
                        number(part, there // cores, there % cores, group),
                    )
                )
            column = group * chips // groups
            between = number(part, column, 0, group)
            aside.append((number(part, 0, 0, group), between))
            across.append((between, number(part - 1, chips - 1, cores - 1, group)))
    axes = QUEUE + ("sp",)
    moved = once_there(resident(lax.ppermute(first, axes, aside)), after)
    return lax.ppermute(first, axes, inside), lax.ppermute(moved, axes, across)


def exchange(block, axes):
    return lax.all_to_all(block, axes, 0, 0)


def per_device(
    spatial_qkv,
    temporal_query,
    temporal_kv,
    timestep,
    noise_level,
    spatial_gate,
    temporal_gate,
    step_table,
):
    x, core = lax.axis_index("x"), lax.axis_index("core")
    x_arg, core_arg = x[None].astype(jnp.int32), core[None].astype(jnp.int32)
    packed, indices = pack(0, spatial_qkv, timestep, noise_level, ())
    early = exchange(packed, "sp")
    indices = shift(indices, QUEUE, -1)
    blocks = spread(x_arg, temporal_query, temporal_kv, packed)
    packed, _ = pack(1, spatial_qkv, timestep, noise_level, blocks[:1])
    between = shift(blocks[3], "x", -1)
    ahead = shift(blocks[2], "x", 2)
    behind = shift(blocks[4], "x", -1)
    beyond = shift(between, "x", -1)
    blocks = [blocks[0], shift(blocks[1], "x", 1), ahead, beyond, behind]
    first = spatial_frame(early, ())
    half = swap_half(core_arg, blocks, (resident(first),))
    late = exchange(once_there(packed, (indices, half)), "sp")
    other = shift(half, "core", 1)
    mine, send = temporal_share(core_arg, blocks, other)
    theirs = shift(send, "core", 1)
    size = lax.axis_size(QUEUE)
    passed = lax.ppermute(
        edge(x_arg, mine, theirs),
        QUEUE,
        [(i, (i - MEMBERS) % size) for i in range(1, size, 2)],
    )
    far, crossed = one_back(first, (resident(mine),))
    near = spatial_frame(late, (resident(mine),))
    back = to_send_back(core_arg, x_arg, mine, theirs, passed, (resident(near),))
    space = exchange(beside(near, far, crossed, (resident(back[0]),)), "sp")
    back = [back[0]] + [shift(back[k], "x", -k) for k in range(1, CHIPS)]
    return combine(
        core_arg, x_arg, space, back, timestep, noise_level, indices,
        spatial_gate, temporal_gate, step_table,
    )


def solution(mesh):
    inner = Mesh(
        mesh.devices.reshape(
            mesh.shape["queue"] // (2 * CHIPS), CHIPS, 2, mesh.shape["sp"]
        ),
        QUEUE + ("sp",),
    )
    return jax.shard_map(
        per_device,
        mesh=inner,
        in_specs=(
            P(QUEUE, None, "sp", None),
            P(QUEUE, "sp", None),
            P(QUEUE, None, "sp", None),
            P(QUEUE),
            P(QUEUE),
            P(),
            P(),
            P(),
        ),
        out_specs=P(QUEUE, "sp", None),
        check_vma=False,
    )
```
